32 devices in a mesh: gx: 8 (over z, y), gy: 4 (over x, core).
Axes of the slice: x: 2, y: 2, z: 4, core: 2. Of those that a mesh axis runs over, the one named last changes fastest.
Arguments:
- atm_state: float32 [2, 72, 512, 512], P(None, None, 'gx', 'gy'), may hold values from -6 to 6
- ocean_state: float32 [2, 60, 512, 512], P(None, None, 'gx', 'gy'), may hold values from -6 to 6
- land_mask: int32 [512, 512], P('gx', 'gy'), may hold values 0 or 1
- elem_op: float32 [16, 16], replicated, may hold values from -1.5 to 1.5
- column_mix: float32 [72, 72], replicated, may hold values from -0.75 to 0.75
- kappa: float32 [2, 60], replicated, may hold values from 0.03 to 0.2
- remap_weight: bfloat16 [512, 4, 4, 128, 128], P('gx', 'gy'), may hold values from -0.5 to 0.5
- intersection: int32 [512, 4, 4], replicated, may hold values from 0 to 2047, as said below
Outputs:
- atm_next: float32 [2, 72, 512, 512], P(None, None, 'gx', 'gy')
- ocean_next: float32 [2, 60, 512, 512], P(None, None, 'gx', 'gy')
- surface_on_atm: float32 [2, 512, 512], P(None, 'gx', 'gy')
The draws below stay inside these ranges and needn't reach their ends.
Inputs may be any that keep to these rules, and one draw needn't show every extreme that they name: `intersection`: among the 256 entries of the atmosphere points of one device (rows of one tile along the first dimension, one column block), at most 20 name blocks of any one ocean tile d = o // 64; in every draw some tile receives exactly 20 from every device.
All inputs are finite; a program needn't handle non-finite values. No bound on the sum of `land_mask` on one device may be relied on, other than what follows from the above.
Results may differ from the reference program's by a relative error of at most 0.0032.
Values may be sent and summed in bfloat16 or wider, within the bound.
A program may use at most 192 MiB of HBM per device.

```python
import math
import jax
import jax.numpy as jnp
from jax import lax

LEV = 72
LO = 60
AX = 64
AY = 128
OX = 64
OY = 128
TOP = 4
OSUB = 2
TILES_X = 8
TILES_Y = 4
TILES = 32
CAP = 20
NAX = 512
NAY = 512
ONX = 512
ONY = 512


def draw_intersection(key, part):
    devices = TILES_X * TILES_Y
    entries = AX * TOP
    slot_count = devices * CAP
    favored = jax.random.randint(jax.random.fold_in(key, 11), (), 0, devices)
    slot_ids = jnp.arange(slot_count, dtype=jnp.int32)
    owners = slot_ids // CAP

    def one_source(source_key):
        subkeys = jax.random.split(source_key, 3)
        shuffled = jax.random.permutation(subkeys[0], slot_count)
        position = jnp.argsort(shuffled).astype(jnp.int32)
        ranking = jnp.where(owners == favored, slot_ids % CAP - CAP, position)
        sorted_slots = jnp.argsort(ranking, stable=True).astype(jnp.int32)
        chosen = sorted_slots[:entries]
        chosen = chosen[jax.random.permutation(subkeys[1], entries)]
        local_row = jax.random.randint(subkeys[2], (entries,), 0, OX)
        return chosen // CAP * OX + local_row
    source_keys = jax.random.split(jax.random.fold_in(key, 12), devices)
    flat_ids = jax.vmap(one_source)(source_keys)
    arranged = jnp.transpose(flat_ids.reshape(TILES_X, TILES_Y, AX, TOP), (0, 2, 1, 3))
    return arranged.reshape(TILES_X * AX, TILES_Y, TOP).astype(jnp.int32)


def set_ends(values, stream_key, smallest, largest):
    longest = values.shape.index(max(values.shape))
    spots = []
    for shift in (0, 1):
        where = [jax.random.randint(jax.random.fold_in(stream_key, axis), (), 0, length) for axis, length in enumerate(values.shape)]
        where[longest] = (where[longest] + shift) % values.shape[longest]
        spots.append(tuple(where))
    return values.at[spots[0]].set(smallest).at[spots[1]].set(largest)


def block_levels(stream_key, shape, pieces, low, top_value):
    factor_of, own = 1.0, jax.random.fold_in(stream_key, 6)
    for axis_at, blocks in pieces:
        steps = jnp.exp(jax.random.uniform(jax.random.fold_in(own, axis_at), (blocks,), jnp.float32, low / len(pieces), top_value / len(pieces)))
        factor_of = factor_of * jnp.repeat(steps, shape[axis_at] // blocks).reshape([-1 if axis == axis_at else 1 for axis in range(len(shape))])
    return factor_of


def gaussian(rng, dims, width, reach, cuts=(), held_as=jnp.bfloat16):
    array = width * jax.random.normal(rng, dims, jnp.float32)
    if cuts:
        array = array * block_levels(rng, dims, cuts, -0.22, 0.18)
    return jnp.clip(array, -reach, reach).astype(held_as)


def setup_inputs(seed: int = 0) -> dict:
    arg_keys = jax.random.split(jax.random.key(seed), 9)
    atm_state = gaussian(arg_keys[0], (2, LEV, NAX, NAY), 1.0, 6.0, ((2, 8), (3, 4)), jnp.float32)
    ocean_state = gaussian(arg_keys[1], (2, LO, ONX, ONY), 1.0, 6.0, ((2, 8), (3, 4)), jnp.float32)
    land_mask = set_ends((jax.random.randint(arg_keys[2], (ONX, ONY), 0, 4) < 3).astype(jnp.int32), jax.random.fold_in(arg_keys[2], 1), 0, 1)
    elem_op = gaussian(arg_keys[3], (16, 16), 16 ** -0.5, 1.5, (), jnp.float32)
    column_mix = gaussian(arg_keys[4], (LEV, LEV), LEV ** -0.5, 0.75, (), jnp.float32)
    kappa = jnp.clip(jnp.exp(jax.random.uniform(arg_keys[5], (2, LO), jnp.float32, math.log(0.03), math.log(0.2))), 0.03, 0.2)
    remap_weight = gaussian(arg_keys[6], (NAX, TILES_Y, TOP, OY, AY), AY ** -0.5, 0.5, ((0, 8), (1, 4)))
    intersection = draw_intersection(jax.random.fold_in(arg_keys[8], 71), 0)
    return dict(atm_state=atm_state, ocean_state=ocean_state, land_mask=land_mask, elem_op=elem_op, column_mix=column_mix, kappa=kappa, remap_weight=remap_weight, intersection=intersection)


ELEM_STEP = 0.5
MIX_STEP = 0.5
FLUX_GAIN = 0.25


def element_step(fields, elem_op, column_mix):
    variables, levels, row_count, col_count = fields.shape
    blocked = fields.reshape(variables, levels, row_count // 4, 4, col_count // 4, 4)
    kernel = elem_op.reshape(4, 4, 4, 4)
    applied = jnp.einsum("abij,vlxiyj->vlxayb", kernel, blocked, precision=lax.Precision.HIGHEST).reshape(fields.shape)
    stepped = fields + ELEM_STEP * applied
    column_term = jnp.einsum("lm,vmxy->vlxy", column_mix, stepped, precision=lax.Precision.HIGHEST)
    return stepped + MIX_STEP * column_term


def edge_average(padded, along):
    inner_count = padded.shape[along] - 2
    center = lax.slice_in_dim(padded, 1, inner_count + 1, axis=along)
    before = lax.slice_in_dim(padded, 0, inner_count, axis=along)
    after = lax.slice_in_dim(padded, 2, inner_count + 2, axis=along)
    place = (jnp.arange(inner_count) % 4).reshape((inner_count,) + (1,) * (padded.ndim - 1 - along))
    return jnp.where(place == 3, (center + after) * 0.5, jnp.where(place == 0, (center + before) * 0.5, center))


def stiffness_sum(padded):
    return edge_average(edge_average(padded, 2), 3)


def ocean_substep(tracers, wet_mask, kappa):
    eastern = jnp.roll(tracers, -1, axis=2)
    western = jnp.roll(tracers, 1, axis=2)
    mask_east = jnp.roll(wet_mask, -1, axis=0)
    mask_west = jnp.roll(wet_mask, 1, axis=0)
    northern = jnp.concatenate([tracers[:, :, :, 1:], jnp.flip(tracers[:, :, :, -1:], axis=2)], axis=3)
    mask_north = jnp.concatenate([wet_mask[:, 1:], jnp.flip(wet_mask[:, -1:], axis=0)], axis=1)
    southern = jnp.concatenate([jnp.zeros_like(tracers[:, :, :, :1]), tracers[:, :, :, :-1]], axis=3)
    mask_south = jnp.concatenate([jnp.zeros_like(wet_mask[:, :1]), wet_mask[:, :-1]], axis=1)
    laplace_sum = mask_east * (eastern - tracers) + mask_west * (western - tracers)
    laplace_sum = laplace_sum + mask_north * (northern - tracers)
    laplace_sum = laplace_sum + mask_south * (southern - tracers)
    return tracers + wet_mask * (kappa[:, :, None, None] * laplace_sum)


def reference(atm_state, ocean_state, land_mask, elem_op, column_mix, kappa, remap_weight, intersection):
    stepped = element_step(atm_state, elem_op, column_mix)
    padded = jnp.pad(stepped, ((0, 0), (0, 0), (1, 1), (1, 1)), mode="wrap")
    atm_next = stiffness_sum(padded)
    surface = atm_next[:, LEV - 1].astype(jnp.bfloat16)
    surface_rows = jnp.transpose(surface.reshape(2, NAX, TILES_Y, AY), (1, 0, 2, 3))

    def forward(pair):
        weight_row, surface_row = pair
        return jnp.einsum("jtqp,fjp->jtfq", weight_row.astype(jnp.float32), surface_row.astype(jnp.float32), precision=lax.Precision.HIGHEST)

    contrib = lax.map(forward, (remap_weight, surface_rows))
    flat_terms = contrib.reshape(-1, 2, OY)
    ocean_ids = intersection.reshape(-1).astype(jnp.int32)
    totals = jnp.zeros((TILES * OX, 2, OY), jnp.float32).at[ocean_ids].add(flat_terms)
    forcing = jnp.transpose(totals.reshape(TILES_X, TILES_Y, OX, 2, OY), (3, 0, 2, 1, 4)).reshape(2, ONX, ONY)
    wet_mask = land_mask.astype(jnp.float32)
    tracers = ocean_state
    for repeat in range(OSUB):
        tracers = ocean_substep(tracers, wet_mask, kappa)
    surface_level = tracers[:, 0] + wet_mask * (FLUX_GAIN * forcing)
    ocean_next = tracers.at[:, 0].set(surface_level)
    sea_surface = ocean_next[:, 0].astype(jnp.bfloat16)
    ocean_blocks = jnp.transpose(sea_surface.reshape(2, TILES_X, OX, TILES_Y, OY), (1, 3, 2, 0, 4)).reshape(TILES * OX, 2, OY)
    entry_values = ocean_blocks[ocean_ids].reshape(NAX, TILES_Y, TOP, 2, OY)

    def backward(pair):
        weight_row, value_row = pair
        return jnp.einsum("jtqp,jtfq->fjp", weight_row.astype(jnp.float32), value_row.astype(jnp.float32), precision=lax.Precision.HIGHEST)

    returned = lax.map(backward, (remap_weight, entry_values))
    surface_on_atm = jnp.transpose(returned, (1, 0, 2, 3)).reshape(2, NAX, NAY)
    return atm_next, ocean_next, surface_on_atm
```

```python
import jax
import jax.numpy as jnp
from jax import lax
from jax.experimental import pallas as pl
from jax.experimental.pallas import tpu as pltpu
from jax.sharding import PartitionSpec as P

OSUB = 2


ELEM_STEP = 0.5
MIX_STEP = 0.5
FLUX_GAIN = 0.25


def row_halo(planes):
    count = lax.axis_size("gx")
    before = lax.ppermute(planes[:, -1], "gx", [(i, (i + 1) % count) for i in range(count)])
    after = lax.ppermute(planes[:, 0], "gx", [((i + 1) % count, i) for i in range(count)])
    return before, after


def col_halo(first, last):
    count = lax.axis_size("gy")
    before = lax.ppermute(last, "gy", [(i, (i + 1) % count) for i in range(count)])
    after = lax.ppermute(first, "gy", [((i + 1) % count, i) for i in range(count)])
    return before, after


def neighbours(x, before, after, axis):
    count = x.shape[axis]
    place = lax.broadcasted_iota(jnp.int32, x.shape, axis)
    down = jnp.where(place == 0, before, pltpu.roll(x, 1, axis))
    up = jnp.where(place == count - 1, after, pltpu.roll(x, count - 1, axis))
    return down, up, place


def averaged(x, before, after, axis):
    down, up, place = neighbours(x, before, after, axis)
    side = place % 4
    return jnp.where(side == 3, (x + up) * 0.5, jnp.where(side == 0, (x + down) * 0.5, x))


def spread_cols(cols_ref, p, x):
    rows, cols = x.shape
    top = lax.broadcasted_iota(jnp.int32, (cols, rows), 0) == 0
    return jnp.where(top, cols_ref[p, 0:1], cols_ref[p, 1:2]).T


def put_edges(edges_ref, p, x):
    turned = x.T
    edges_ref[p, 0:1] = turned[0:1]
    edges_ref[p, 1:2] = turned[x.shape[1] - 1 :]


def edges_kernel(x_ref, edges_ref):
    for p in range(x_ref.shape[0]):
        put_edges(edges_ref, p, x_ref[p])


def stiffness_kernel(x_ref, west_ref, east_ref, cols_ref, out_ref):
    for p in range(x_ref.shape[0]):
        x = averaged(x_ref[p], west_ref[p], east_ref[p], 0)
        sides = spread_cols(cols_ref, p, x)
        out_ref[p] = averaged(x, sides, sides, 1)


def tracer_kernel(x_ref, west_ref, east_ref, cols_ref, masks_ref, kappa_ref, out_ref, *edges):
    for p in range(x_ref.shape[0]):
        x = x_ref[p]
        sides = spread_cols(cols_ref, p, x)
        western, eastern, _ = neighbours(x, west_ref[p], east_ref[p], 0)
        southern, northern, _ = neighbours(x, sides, sides, 1)
        total = masks_ref[0] * (eastern - x) + masks_ref[1] * (western - x)
        total = total + masks_ref[2] * (northern - x)
        total = total + masks_ref[3] * (southern - x)
        result = x + masks_ref[4] * (kappa_ref[p] * total)
        out_ref[p] = result
        if edges:
            put_edges(edges[0], p, result)


def plane_call(kernel, x, sides=(), extras=(), fill=True, edges=False):
    planes, rows, cols = x.shape
    step = 12 if planes % 12 == 0 else 1
    block = lambda *dims: pl.BlockSpec((step,) + dims, lambda i: (i, 0, 0))
    specs = [block(rows, cols)]
    args = [x]
    if sides:
        west, east, south, north = sides
        specs += [block(1, cols), block(1, cols), block(2, rows)]
        args += [west[:, None], east[:, None], jnp.stack([south, north], axis=1)]
    if extras:
        masks, scale = extras
        specs += [pl.BlockSpec(masks.shape, lambda i: (0, 0, 0)), block(1, cols)]
        args += [masks, scale]
    out_specs = [block(rows, cols)] * fill + [block(2, rows)] * edges
    out_shape = [jax.ShapeDtypeStruct(x.shape, x.dtype)] * fill
    out_shape += [jax.ShapeDtypeStruct((planes, 2, rows), x.dtype)] * edges
    return pl.pallas_call(
        kernel,
        grid=(planes // step,),
        in_specs=specs,
        out_specs=out_specs,
        out_shape=out_shape,
        compiler_params=pltpu.CompilerParams(vmem_limit_bytes=32 * 1024 * 1024),
    )(*args)


def split(x):
    high = x.astype(jnp.bfloat16)
    return high, (x - high.astype(jnp.float32)).astype(jnp.bfloat16)


def dot(a, b):
    return jnp.dot(a, b, preferred_element_type=jnp.float32)


def element_kernel(x_ref, op_ref, mix_ref, out_ref, held, stepped, spread_ref):
    _, levels, rows, cols = x_ref.shape
    wide = 4 * cols

    @pl.when((pl.program_id(0) == 0) & (pl.program_id(1) == 0))
    def _():
        def place(index):
            return index // cols * 4 + index % 4

        tall = place(lax.broadcasted_iota(jnp.int32, (wide, 16), 0))
        left = (tall == lax.broadcasted_iota(jnp.int32, (wide, 16), 1)).astype(jnp.float32)
        flat = place(lax.broadcasted_iota(jnp.int32, (16, wide), 1))
        right = (flat == lax.broadcasted_iota(jnp.int32, (16, wide), 0)).astype(jnp.float32)
        row = lax.broadcasted_iota(jnp.int32, (wide, wide), 0) % cols // 4
        col = lax.broadcasted_iota(jnp.int32, (wide, wide), 1) % cols // 4
        for k, piece in enumerate(split(op_ref[...])):
            half = dot(left, piece.astype(jnp.float32))
            full = dot(half, right)
            spread_ref[k] = jnp.where(row == col, full, 0.0).astype(jnp.bfloat16)

    held[...] = x_ref[0].reshape(levels * rows, cols)
    quarter = levels * rows // 4
    parts = [held[pl.ds(i, quarter, stride=4), :] for i in range(4)]
    high, low = split(jnp.concatenate(parts, axis=1))
    applied = dot(high, spread_ref[0]) + (dot(low, spread_ref[0]) + dot(high, spread_ref[1]))
    for i in range(4):
        stepped[pl.ds(i, quarter, stride=4), :] = (
            parts[i] + ELEM_STEP * applied[:, i * cols : (i + 1) * cols]
        )
    lines = [stepped[pl.ds(r, levels, stride=rows), :] for r in range(rows)]
    high, low = split(jnp.concatenate(lines, axis=1))
    mix_high, mix_low = split(mix_ref[...])
    mixed = dot(mix_high, high) + (dot(mix_low, high) + dot(mix_high, low))
    for r in range(rows):
        held[pl.ds(r, levels, stride=rows), :] = (
            lines[r] + MIX_STEP * mixed[:, r * cols : (r + 1) * cols]
        )
    out_ref[0] = held[...].reshape(levels, rows, cols)


def element_step(fields, elem_op, column_mix):
    variables, levels, row_count, col_count = fields.shape
    rows = 8
    block = pl.BlockSpec((1, levels, rows, col_count), lambda v, r: (v, 0, r, 0))
    return pl.pallas_call(
        element_kernel,
        grid=(variables, row_count // rows),
        in_specs=[
            block,
            pl.BlockSpec(elem_op.shape, lambda v, r: (0, 0)),
            pl.BlockSpec(column_mix.shape, lambda v, r: (0, 0)),
        ],
        out_specs=block,
        out_shape=jax.ShapeDtypeStruct(fields.shape, fields.dtype),
        scratch_shapes=[pltpu.VMEM((levels * rows, col_count), jnp.float32)] * 2
        + [pltpu.VMEM((2, 4 * col_count, 4 * col_count), jnp.bfloat16)],
        compiler_params=pltpu.CompilerParams(vmem_limit_bytes=32 * 1024 * 1024),
    )(fields, elem_op.T, column_mix)


def column_average(column, before, after):
    padded = jnp.concatenate([before[:, None], column, after[:, None]], axis=1)
    side = jnp.arange(column.shape[1])[None, :] % 4
    return jnp.where(
        side == 3,
        (column + padded[:, 2:]) * 0.5,
        jnp.where(side == 0, (column + padded[:, :-2]) * 0.5, column),
    )


def stiffness_sum(stepped):
    x = stepped.reshape((-1,) + stepped.shape[2:])
    west, east = row_halo(x)
    (edges,) = plane_call(edges_kernel, x, fill=False, edges=True)
    first = column_average(edges[:, 0], west[:, 0], east[:, 0])
    last = column_average(edges[:, 1], west[:, -1], east[:, -1])
    south, north = col_halo(first, last)
    (out,) = plane_call(stiffness_kernel, x, (west, east, south, north))
    return out.reshape(stepped.shape)


def ocean_halo(x, first, last, gy_index, gy_count):
    count = lax.axis_size("gx")
    west, east = row_halo(x)
    south, north = col_halo(first, last)
    mirrored = lax.ppermute(last, "gx", [(i, count - 1 - i) for i in range(count)])
    north = jnp.where(gy_index == gy_count - 1, jnp.flip(mirrored, axis=1), north)
    return west, east, south, north


def mask_set(wet, gy_index, gy_count):
    west, east, south, north = (side[0] for side in ocean_halo(wet[None], wet[None, :, 0], wet[None, :, -1], gy_index, gy_count))
    south = jnp.where(gy_index == 0, jnp.zeros_like(south), south)
    return jnp.stack(
        [
            jnp.concatenate([wet[1:], east[None]], axis=0),
            jnp.concatenate([west[None], wet[:-1]], axis=0),
            jnp.concatenate([wet[:, 1:], north[:, None]], axis=1),
            jnp.concatenate([south[:, None], wet[:, :-1]], axis=1),
            wet,
        ]
    )


def tracer_steps(tracers, masks, kappa, gy_index, gy_count):
    x = tracers.reshape((-1,) + tracers.shape[2:])
    scale = jnp.broadcast_to(kappa.reshape(-1, 1, 1), (x.shape[0], 1, x.shape[2]))
    (edges,) = plane_call(edges_kernel, x, fill=False, edges=True)
    for repeat in range(OSUB):
        halo = ocean_halo(x, edges[:, 0], edges[:, 1], gy_index, gy_count)
        if repeat < OSUB - 1:
            x, edges = plane_call(tracer_kernel, x, halo, (masks, scale), edges=True)
        else:
            (x,) = plane_call(tracer_kernel, x, halo, (masks, scale))
    return x.reshape(tracers.shape)


def per_device(
    atm_state, ocean_state, land_mask, elem_op, column_mix, kappa, remap_weight, intersection
):
    gx_count = lax.axis_size("gx")
    gy_count = lax.axis_size("gy")
    tile_count = gx_count * gy_count
    gx_index = lax.axis_index("gx")
    gy_index = lax.axis_index("gy")
    levels = atm_state.shape[1]
    atm_rows = atm_state.shape[2]
    ocean_rows = ocean_state.shape[2]
    ocean_cols = ocean_state.shape[3]
    intersections = remap_weight.shape[2]
    entries = atm_rows * intersections
    capacity = max(2, 5 * entries // (2 * tile_count))
    slot_total = tile_count * capacity
    stepped = element_step(atm_state, elem_op, column_mix)
    atm_next = stiffness_sum(stepped)
    surface = atm_next[:, levels - 1].astype(jnp.bfloat16)
    weights = remap_weight[:, 0]
    products = lax.dot_general(
        weights, surface, (((3,), (2,)), ((0,), (1,))), preferred_element_type=jnp.float32
    )
    contrib = jnp.transpose(products, (0, 1, 3, 2)).reshape(entries, 2, ocean_cols)
    own_ids = lax.dynamic_slice(
        intersection, (gx_index * atm_rows, gy_index, jnp.int32(0)), (atm_rows, 1, intersections)
    ).reshape(entries)
    target_dev = own_ids // ocean_rows
    entry_order = jnp.arange(entries)
    earlier_same = (target_dev[None, :] == target_dev[:, None]) & (
        entry_order[None, :] < entry_order[:, None]
    )
    slot_rank = jnp.sum(earlier_same.astype(jnp.int32), axis=1)
    slot_pos = target_dev * capacity + slot_rank
    send_map = (slot_pos[:, None] == jnp.arange(slot_total)[None, :]).astype(jnp.float32)
    outgoing = jnp.einsum("es,efq->sfq", send_map, contrib, precision=lax.Precision.HIGHEST)
    all_ids = jnp.transpose(
        intersection.reshape(gx_count, atm_rows, gy_count, intersections), (0, 2, 1, 3)
    ).reshape(tile_count, entries)
    own_tile = gx_index * gy_count + gy_index
    hits = (all_ids // ocean_rows == own_tile).astype(jnp.int32)
    recv_rank = jnp.cumsum(hits, axis=1) - hits
    slot_pick = (
        hits[:, :, None] * (recv_rank[:, :, None] == jnp.arange(capacity)).astype(jnp.int32)
    ).astype(jnp.float32)
    row_pick = (all_ids[:, :, None] % ocean_rows == jnp.arange(ocean_rows)).astype(jnp.float32)
    receive_map = jnp.einsum(
        "sek,sel->lsk", slot_pick, row_pick, precision=lax.Precision.HIGHEST
    ).reshape(ocean_rows, slot_total)
    incoming = lax.all_to_all(
        outgoing.reshape(tile_count, capacity, 2, ocean_cols),
        ("gx", "gy"),
        split_axis=0,
        concat_axis=0,
        tiled=True,
    )
    forcing = jnp.einsum(
        "lc,cfq->flq",
        receive_map,
        incoming.reshape(slot_total, 2, ocean_cols),
        precision=lax.Precision.HIGHEST,
    )
    wet_mask = land_mask.astype(jnp.float32)
    masks = mask_set(wet_mask, gy_index, gy_count)
    tracers = tracer_steps(ocean_state, masks, kappa, gy_index, gy_count)
    surface_level = tracers[:, 0] + wet_mask * (FLUX_GAIN * forcing)
    ocean_next = tracers.at[:, 0].set(surface_level)
    sea_surface = ocean_next[:, 0].astype(jnp.bfloat16)
    back_out = jnp.einsum(
        "lc,flq->cfq",
        receive_map.astype(jnp.bfloat16),
        sea_surface,
        preferred_element_type=jnp.float32,
    ).astype(jnp.bfloat16)
    back_in = lax.all_to_all(
        back_out.reshape(tile_count, capacity, 2, ocean_cols),
        ("gx", "gy"),
        split_axis=0,
        concat_axis=0,
        tiled=True,
    )
    entry_values = jnp.einsum(
        "es,sfq->efq",
        send_map.astype(jnp.bfloat16),
        back_in.reshape(slot_total, 2, ocean_cols),
        preferred_element_type=jnp.float32,
    )
    entry_values = entry_values.astype(jnp.bfloat16).reshape(atm_rows, intersections, 2, ocean_cols)
    returned = lax.dot_general(
        weights, entry_values, (((1, 2), (1, 3)), ((0,), (0,))), preferred_element_type=jnp.float32
    )
    surface_on_atm = jnp.transpose(returned, (2, 0, 1))
    return (atm_next, ocean_next, surface_on_atm)


def solution(mesh):
    placed = (
        P(None, None, "gx", "gy"),
        P(None, None, "gx", "gy"),
        P("gx", "gy"),
        P(),
        P(),
        P(),
        P("gx", "gy", None, None, None),
        P(),
    )
    return jax.shard_map(
        per_device,
        mesh=mesh,
        in_specs=placed,
        out_specs=(P(None, None, "gx", "gy"), P(None, None, "gx", "gy"), P(None, "gx", "gy")),
        check_vma=False,
    )
```

```python
import jax
import jax.numpy as jnp
from jax import lax
from jax.experimental import pallas as pl
from jax.experimental.pallas import tpu as pltpu
from jax.sharding import PartitionSpec as P

OSUB = 2


ELEM_STEP = 0.5
MIX_STEP = 0.5
FLUX_GAIN = 0.25


def row_halo(first, last):
    count = lax.axis_size("gx")
    before = lax.ppermute(last, "gx", [(i, (i + 1) % count) for i in range(count)])
    after = lax.ppermute(first, "gx", [((i + 1) % count, i) for i in range(count)])
    return before, after


def col_halo(first, last):
    count = lax.axis_size("gy")
    before = lax.ppermute(last, "gy", [(i, (i + 1) % count) for i in range(count)])
    after = lax.ppermute(first, "gy", [((i + 1) % count, i) for i in range(count)])
    return before, after


def neighbours(x, before, after, axis):
    count = x.shape[axis]
    place = lax.broadcasted_iota(jnp.int32, x.shape, axis)
    down = jnp.where(place == 0, before, pltpu.roll(x, 1, axis))
    up = jnp.where(place == count - 1, after, pltpu.roll(x, count - 1, axis))
    return down, up, place


def averaged(x, before, after, axis):
    down, up, place = neighbours(x, before, after, axis)
    side = place % 4
    return jnp.where(side == 3, (x + up) * 0.5, jnp.where(side == 0, (x + down) * 0.5, x))


def spread_cols(cols_ref, p, x):
    rows, cols = x.shape
    top = lax.broadcasted_iota(jnp.int32, (cols, rows), 0) == 0
    return jnp.where(top, cols_ref[p, 0:1], cols_ref[p, 1:2]).T


def put_edges(edges_ref, lines_ref, p, x):
    lines_ref[p, 0:1] = x[0:1]
    lines_ref[p, 1:2] = x[x.shape[0] - 1 :]
    turned = x.T
    edges_ref[p, 0:1] = turned[0:1]
    edges_ref[p, 1:2] = turned[x.shape[1] - 1 :]


def edges_kernel(x_ref, edges_ref, lines_ref):
    for p in range(x_ref.shape[0]):
        put_edges(edges_ref, lines_ref, p, x_ref[p])


def stiffness_kernel(x_ref, west_ref, east_ref, cols_ref, out_ref):
    for p in range(x_ref.shape[0]):
        x = averaged(x_ref[p], west_ref[p], east_ref[p], 0)
        sides = spread_cols(cols_ref, p, x)
        out_ref[p] = averaged(x, sides, sides, 1)


def tracer_kernel(x_ref, west_ref, east_ref, cols_ref, masks_ref, kappa_ref, out_ref, *edges):
    for p in range(x_ref.shape[0]):
        x = x_ref[p]
        sides = spread_cols(cols_ref, p, x)
        western, eastern, _ = neighbours(x, west_ref[p], east_ref[p], 0)
        southern, northern, _ = neighbours(x, sides, sides, 1)
        total = masks_ref[0] * (eastern - x) + masks_ref[1] * (western - x)
        total = total + masks_ref[2] * (northern - x)
        total = total + masks_ref[3] * (southern - x)
        result = x + masks_ref[4] * (kappa_ref[p] * total)
        out_ref[p] = result
        if edges:
            put_edges(*edges, p, result)


def plane_call(kernel, x, sides=(), extras=(), fill=True, edges=False):
    planes, rows, cols = x.shape
    step = 12 if planes % 12 == 0 else 1
    block = lambda *dims: pl.BlockSpec((step,) + dims, lambda i: (i, 0, 0))
    specs = [block(rows, cols)]
    args = [x]
    if sides:
        west, east, south, north = sides
        specs += [block(1, cols), block(1, cols), block(2, rows)]
        args += [west[:, None], east[:, None], jnp.stack([south, north], axis=1)]
    if extras:
        masks, scale = extras
        specs += [pl.BlockSpec(masks.shape, lambda i: (0, 0, 0)), block(1, cols)]
        args += [masks, scale]
    out_specs = [block(rows, cols)] * fill + [block(2, rows), block(2, cols)] * edges
    out_shape = [jax.ShapeDtypeStruct(x.shape, x.dtype)] * fill
    out_shape += [jax.ShapeDtypeStruct((planes, 2, side), x.dtype) for side in (rows, cols)] * edges
    return pl.pallas_call(
        kernel,
        grid=(planes // step,),
        in_specs=specs,
        out_specs=out_specs,
        out_shape=out_shape,
        cost_estimate=pl.CostEstimate(flops=30 * x.size, bytes_accessed=8 * x.size, transcendentals=0),
        compiler_params=pltpu.CompilerParams(vmem_limit_bytes=32 * 1024 * 1024),
    )(*args)


def split(x):
    high = x.astype(jnp.bfloat16)
    return high, (x - high.astype(jnp.float32)).astype(jnp.bfloat16)


def dot(a, b):
    return jnp.dot(a, b, preferred_element_type=jnp.float32)


def element_kernel(x_ref, op_ref, mix_ref, out_ref, held, stepped, spread_ref):
    _, levels, rows, cols = x_ref.shape
    wide = 4 * cols

    @pl.when((pl.program_id(0) == 0) & (pl.program_id(1) == 0))
    def _():
        def place(index):
            return index // cols * 4 + index % 4

        tall = place(lax.broadcasted_iota(jnp.int32, (wide, 16), 0))
        left = (tall == lax.broadcasted_iota(jnp.int32, (wide, 16), 1)).astype(jnp.float32)
        flat = place(lax.broadcasted_iota(jnp.int32, (16, wide), 1))
        right = (flat == lax.broadcasted_iota(jnp.int32, (16, wide), 0)).astype(jnp.float32)
        row = lax.broadcasted_iota(jnp.int32, (wide, wide), 0) % cols // 4
        col = lax.broadcasted_iota(jnp.int32, (wide, wide), 1) % cols // 4
        for k, piece in enumerate(split(op_ref[...])):
            half = dot(left, piece.astype(jnp.float32))
            full = dot(half, right)
            spread_ref[k] = jnp.where(row == col, full, 0.0).astype(jnp.bfloat16)

    held[...] = x_ref[0].reshape(levels * rows, cols)
    quarter = levels * rows // 4
    parts = [held[pl.ds(i, quarter, stride=4), :] for i in range(4)]
    high, low = split(jnp.concatenate(parts, axis=1))
    applied = dot(high, spread_ref[0]) + (dot(low, spread_ref[0]) + dot(high, spread_ref[1]))
    for i in range(4):
        stepped[pl.ds(i, quarter, stride=4), :] = (
            parts[i] + ELEM_STEP * applied[:, i * cols : (i + 1) * cols]
        )
    lines = [stepped[pl.ds(r, levels, stride=rows), :] for r in range(rows)]
    high, low = split(jnp.concatenate(lines, axis=1))
    mix_high, mix_low = split(mix_ref[...])
    mixed = dot(mix_high, high) + (dot(mix_low, high) + dot(mix_high, low))
    for r in range(rows):
        held[pl.ds(r, levels, stride=rows), :] = (
            lines[r] + MIX_STEP * mixed[:, r * cols : (r + 1) * cols]
        )
    out_ref[0] = held[...].reshape(levels, rows, cols)


def element_step(fields, elem_op, column_mix):
    variables, levels, row_count, col_count = fields.shape
    rows = 8
    block = pl.BlockSpec((1, levels, rows, col_count), lambda v, r: (v, 0, r, 0))
    return pl.pallas_call(
        element_kernel,
        grid=(variables, row_count // rows),
        in_specs=[
            block,
            pl.BlockSpec(elem_op.shape, lambda v, r: (0, 0)),
            pl.BlockSpec(column_mix.shape, lambda v, r: (0, 0)),
        ],
        out_specs=block,
        out_shape=jax.ShapeDtypeStruct(fields.shape, fields.dtype),
        scratch_shapes=[pltpu.VMEM((levels * rows, col_count), jnp.float32)] * 2
        + [pltpu.VMEM((2, 4 * col_count, 4 * col_count), jnp.bfloat16)],
        compiler_params=pltpu.CompilerParams(vmem_limit_bytes=32 * 1024 * 1024),
    )(fields, elem_op.T, column_mix)


def column_average(column, before, after):
    padded = jnp.concatenate([before[:, None], column, after[:, None]], axis=1)
    side = jnp.arange(column.shape[1])[None, :] % 4
    return jnp.where(
        side == 3,
        (column + padded[:, 2:]) * 0.5,
        jnp.where(side == 0, (column + padded[:, :-2]) * 0.5, column),
    )


def stiffness_sum(stepped):
    x = stepped.reshape((-1,) + stepped.shape[2:])
    edges, lines = plane_call(edges_kernel, x, fill=False, edges=True)
    west, east = row_halo(lines[:, 0], lines[:, 1])
    first = column_average(edges[:, 0], west[:, 0], east[:, 0])
    last = column_average(edges[:, 1], west[:, -1], east[:, -1])
    south, north = col_halo(first, last)
    halo = (west, east, south, north)
    levels = stepped.shape[1]
    (surface,) = plane_call(
        stiffness_kernel, x[levels - 1 :: levels], [side[levels - 1 :: levels] for side in halo]
    )
    (out,) = plane_call(stiffness_kernel, x, halo)
    return out.reshape(stepped.shape), surface


def ocean_halo(edges, lines, gy_index, gy_count):
    count = lax.axis_size("gx")
    first, last = edges[:, 0], edges[:, 1]
    west, east = row_halo(lines[:, 0], lines[:, 1])
    south, north = col_halo(first, last)
    mirrored = lax.ppermute(last, "gx", [(i, count - 1 - i) for i in range(count)])
    north = jnp.where(gy_index == gy_count - 1, jnp.flip(mirrored, axis=1), north)
    return west, east, south, north


def mask_set(wet, gy_index, gy_count):
    edges = jnp.stack([wet[:, 0], wet[:, -1]])[None]
    lines = jnp.stack([wet[0], wet[-1]])[None]
    west, east, south, north = (side[0] for side in ocean_halo(edges, lines, gy_index, gy_count))
    south = jnp.where(gy_index == 0, jnp.zeros_like(south), south)
    return jnp.stack(
        [
            jnp.concatenate([wet[1:], east[None]], axis=0),
            jnp.concatenate([west[None], wet[:-1]], axis=0),
            jnp.concatenate([wet[:, 1:], north[:, None]], axis=1),
            jnp.concatenate([south[:, None], wet[:, :-1]], axis=1),
            wet,
        ]
    )


def tracer_steps(tracers, masks, kappa, gy_index, gy_count):
    x = tracers.reshape((-1,) + tracers.shape[2:])
    scale = jnp.broadcast_to(kappa.reshape(-1, 1, 1), (x.shape[0], 1, x.shape[2]))
    edges, lines = plane_call(edges_kernel, x, fill=False, edges=True)
    for repeat in range(OSUB):
        halo = ocean_halo(edges, lines, gy_index, gy_count)
        if repeat < OSUB - 1:
            x, edges, lines = plane_call(tracer_kernel, x, halo, (masks, scale), edges=True)
        else:
            levels = tracers.shape[1]
            (top,) = plane_call(
                tracer_kernel, x[::levels], [side[::levels] for side in halo], (masks, scale[::levels])
            )
            (x,) = plane_call(tracer_kernel, x, halo, (masks, scale))
    return x.reshape(tracers.shape), top


def per_device(
    atm_state, ocean_state, land_mask, elem_op, column_mix, kappa, remap_weight, intersection
):
    gx_count = lax.axis_size("gx")
    gy_count = lax.axis_size("gy")
    tile_count = gx_count * gy_count
    gx_index = lax.axis_index("gx")
    gy_index = lax.axis_index("gy")
    levels = atm_state.shape[1]
    atm_rows = atm_state.shape[2]
    ocean_rows = ocean_state.shape[2]
    ocean_cols = ocean_state.shape[3]
    intersections = remap_weight.shape[2]
    entries = atm_rows * intersections
    capacity = max(2, 5 * entries // (2 * tile_count))
    slot_total = tile_count * capacity
    stepped = element_step(atm_state, elem_op, column_mix)
    atm_next, surface = stiffness_sum(stepped)
    surface = surface.astype(jnp.bfloat16)
    weights = remap_weight[:, 0]
    products = lax.dot_general(
        weights, surface, (((3,), (2,)), ((0,), (1,))), preferred_element_type=jnp.float32
    )
    contrib = jnp.transpose(products, (0, 1, 3, 2)).reshape(entries, 2, ocean_cols)
    own_ids = lax.dynamic_slice(
        intersection, (gx_index * atm_rows, gy_index, jnp.int32(0)), (atm_rows, 1, intersections)
    ).reshape(entries)
    target_dev = own_ids // ocean_rows
    entry_order = jnp.arange(entries)
    earlier_same = (target_dev[None, :] == target_dev[:, None]) & (
        entry_order[None, :] < entry_order[:, None]
    )
    slot_rank = jnp.sum(earlier_same.astype(jnp.int32), axis=1)
    slot_pos = target_dev * capacity + slot_rank
    send_map = (slot_pos[:, None] == jnp.arange(slot_total)[None, :]).astype(jnp.float32)
    outgoing = jnp.einsum("es,efq->sfq", send_map, contrib, precision=lax.Precision.HIGHEST)
    all_ids = jnp.transpose(
        intersection.reshape(gx_count, atm_rows, gy_count, intersections), (0, 2, 1, 3)
    ).reshape(tile_count, entries)
    own_tile = gx_index * gy_count + gy_index
    hits = (all_ids // ocean_rows == own_tile).astype(jnp.int32)
    recv_rank = jnp.cumsum(hits, axis=1) - hits
    slot_pick = (
        hits[:, :, None] * (recv_rank[:, :, None] == jnp.arange(capacity)).astype(jnp.int32)
    ).astype(jnp.float32)
    row_pick = (all_ids[:, :, None] % ocean_rows == jnp.arange(ocean_rows)).astype(jnp.float32)
    receive_map = jnp.einsum(
        "sek,sel->lsk", slot_pick, row_pick, precision=lax.Precision.HIGHEST
    ).reshape(ocean_rows, slot_total)
    incoming = lax.all_to_all(
        outgoing.reshape(tile_count, capacity, 2, ocean_cols),
        ("gx", "gy"),
        split_axis=0,
        concat_axis=0,
        tiled=True,
    )
    forcing = jnp.einsum(
        "lc,cfq->flq",
        receive_map,
        incoming.reshape(slot_total, 2, ocean_cols),
        precision=lax.Precision.HIGHEST,
    )
    wet_mask = land_mask.astype(jnp.float32)
    masks = mask_set(wet_mask, gy_index, gy_count)
    tracers, top = tracer_steps(ocean_state, masks, kappa, gy_index, gy_count)
    surface_level = top + wet_mask * (FLUX_GAIN * forcing)
    ocean_next = tracers.at[:, 0].set(surface_level)
    sea_surface = surface_level.astype(jnp.bfloat16)
    back_out = jnp.einsum(
        "lc,flq->cfq",
        receive_map.astype(jnp.bfloat16),
        sea_surface,
        preferred_element_type=jnp.float32,
    ).astype(jnp.bfloat16)
    back_in = lax.all_to_all(
        back_out.reshape(tile_count, capacity, 2, ocean_cols),
        ("gx", "gy"),
        split_axis=0,
        concat_axis=0,
        tiled=True,
    )
    entry_values = jnp.einsum(
        "es,sfq->efq",
        send_map.astype(jnp.bfloat16),
        back_in.reshape(slot_total, 2, ocean_cols),
        preferred_element_type=jnp.float32,
    )
    entry_values = entry_values.astype(jnp.bfloat16).reshape(atm_rows, intersections, 2, ocean_cols)
    returned = lax.dot_general(
        weights, entry_values, (((1, 2), (1, 3)), ((0,), (0,))), preferred_element_type=jnp.float32
    )
    surface_on_atm = jnp.transpose(returned, (2, 0, 1))
    return (atm_next, ocean_next, surface_on_atm)


def solution(mesh):
    placed = (
        P(None, None, "gx", "gy"),
        P(None, None, "gx", "gy"),
        P("gx", "gy"),
        P(),
        P(),
        P(),
        P("gx", "gy", None, None, None),
        P(),
    )
    return jax.shard_map(
        per_device,
        mesh=mesh,
        in_specs=placed,
        out_specs=(P(None, None, "gx", "gy"), P(None, None, "gx", "gy"), P(None, "gx", "gy")),
        check_vma=False,
    )
```
